256 devices in a mesh: ctx: 64 (over y, x_hi, z), head: 4 (over x_lo, core).
Axes of the slice: x: 4 (x_hi: 2, x_lo: 2; x = x_hi * 2 + x_lo), y: 4, z: 8, core: 2. Of those that a mesh axis runs over, the one named last changes fastest.
Arguments:
- query: bfloat16 [65536, 4096], P('ctx', 'head'), may hold values from -6 to 6
- key: bfloat16 [65536, 4096], P('ctx', 'head'), may hold values from -6 to 6
- value: bfloat16 [65536, 4096], P('ctx', 'head'), may hold values from -6 to 6
- windows: int32 [4096], P('ctx'), may hold values from 1 to 4, as said below
- out_weight: bfloat16 [4096, 4096], P(None, 'head'), may hold values from -0.09375 to 0.09375
Outputs:
- mixed: bfloat16 [65536, 4096], P('ctx', 'head')
The draws below stay inside these ranges and needn't reach their ends.
Inputs may be any that keep to these rules, and one draw needn't show every extreme that they name: `windows`: both ends are reached in every draw.
All inputs are finite; a program needn't handle non-finite values.
Results may differ from the reference program's by a relative error of at most 0.0095.
Values may be sent and summed in bfloat16 or wider, within the bound.
No kernel may reach another device: no remote copies, remote signals or barrier semaphores. Data moves between devices by JAX's collectives and lax.ppermute only.
A program may use at most 128 MiB of HBM per device.

```python
import jax
import jax.numpy as jnp
from jax import lax

H = 32
HD = 128
D = 4096
G = 16
WMAX = 4
TOKENS = 65536
CELLS = 4096
COARSE = 256


def layered(key):
    coarse_key, cell_key, token_key = jax.random.split(key, 3)
    coarse_part = jnp.repeat(jax.random.normal(coarse_key, (COARSE, D), jnp.float32), G * G, axis=0)
    cell_part = jnp.repeat(jax.random.normal(cell_key, (CELLS, D), jnp.float32), G, axis=0)
    token_part = jax.random.normal(token_key, (TOKENS, D), jnp.float32)
    return 0.6 * (coarse_part + cell_part + token_part)


def draw_query(key, part):
    key = jax.random.fold_in(key, 1)
    drawn = jax.random.normal(key, (TOKENS, D), jnp.float32)
    return jnp.clip(drawn, -6.0, 6.0).astype(jnp.bfloat16)


def draw_key(key, part):
    key = jax.random.fold_in(key, 2)
    drawn = layered(key)
    return jnp.clip(drawn, -6.0, 6.0).astype(jnp.bfloat16)


def draw_value(key, part):
    key = jax.random.fold_in(key, 3)
    drawn = layered(key)
    return jnp.clip(drawn, -6.0, 6.0).astype(jnp.bfloat16)


def draw_windows(key, part):
    key = jax.random.fold_in(key, 4)
    first_key, second_key, third_key = jax.random.split(key, 3)
    drawn = jax.random.randint(first_key, (CELLS,), 1, WMAX + 1, jnp.int32)
    spots = jnp.arange(CELLS, dtype=jnp.int32)
    high_spot = jax.random.randint(second_key, (), 0, CELLS, jnp.int32)
    low_spot = (high_spot + 1 + jax.random.randint(third_key, (), 0, CELLS - 1, jnp.int32)) % CELLS
    drawn = jnp.where(spots == high_spot, WMAX, drawn)
    drawn = jnp.where(spots == low_spot, 1, drawn)
    return drawn.astype(jnp.int32)


def block_scale(rng, dims, shards, least, top_value):
    loudness = 1.0
    for dim, shards_of in shards:
        heights = jax.random.uniform(jax.random.fold_in(jax.random.fold_in(rng, 6), dim), (shards_of,), jnp.float32, least / len(shards), top_value / len(shards))
        loudness = loudness * jnp.repeat(jnp.exp(heights), dims[dim] // shards_of).reshape((-1,) + (1,) * (len(dims) - 1 - dim))
    return loudness


def noise(rng, extent, scale, limit, shards=(), kind=jnp.bfloat16):
    entries = scale * jax.random.normal(rng, extent, jnp.float32)
    if shards:
        entries = entries * block_scale(rng, extent, shards, -0.22, 0.18)
    return jnp.clip(entries, -limit, limit).astype(kind)


def setup_inputs(seed: int = 0) -> dict:
    streams_of = jax.random.split(jax.random.key(seed), 6)
    return {
        "query": draw_query(jax.random.fold_in(streams_of[5], 71), 0),
        "key": draw_key(jax.random.fold_in(streams_of[5], 71), 0),
        "value": draw_value(jax.random.fold_in(streams_of[5], 71), 0),
        "windows": draw_windows(jax.random.fold_in(streams_of[5], 71), 0),
        "out_weight": noise(streams_of[4], (D, D), D ** -0.5, 0.09375, ((1, 4),)),
    }


def pooled(array, width):
    rows_total = array.shape[0]
    summed = jnp.sum(array.astype(jnp.float32).reshape(rows_total // width, width, array.shape[1]), axis=1)
    return (summed / width).astype(jnp.bfloat16)


def scored(queries, keys_block, mask):
    values_f = jnp.einsum("qhe,khe->hqk", queries.astype(jnp.float32), keys_block.astype(jnp.float32))
    values_f = values_f * (HD ** -0.5)
    return jnp.where(mask[None, :, :], values_f, -jnp.inf)


def reference(query, key, value, windows, out_weight):
    key1 = pooled(key, G)
    value1 = pooled(value, G)
    key2 = pooled(key, G * G)
    value2 = pooled(value, G * G)
    halo_rows = WMAX * G
    key_pad = jnp.concatenate([jnp.zeros((halo_rows, D), jnp.bfloat16), key], axis=0)
    value_pad = jnp.concatenate([jnp.zeros((halo_rows, D), jnp.bfloat16), value], axis=0)
    key1_pad = jnp.concatenate([jnp.zeros((G, D), jnp.bfloat16), key1], axis=0)
    value1_pad = jnp.concatenate([jnp.zeros((G, D), jnp.bfloat16), value1], axis=0)
    block_rows = G * G

    def one_block(block):
        first = block * block_rows
        rows_q = lax.dynamic_slice_in_dim(query, first, block_rows, 0).reshape(block_rows, H, HD)
        near_k = lax.dynamic_slice_in_dim(key_pad, first, block_rows + halo_rows, 0).reshape(-1, H, HD)
        near_v = lax.dynamic_slice_in_dim(value_pad, first, block_rows + halo_rows, 0).reshape(-1, H, HD)
        mid_k = lax.dynamic_slice_in_dim(key1_pad, block * G, 2 * G, 0).reshape(-1, H, HD)
        mid_v = lax.dynamic_slice_in_dim(value1_pad, block * G, 2 * G, 0).reshape(-1, H, HD)
        far_k = key2.reshape(-1, H, HD)
        far_v = value2.reshape(-1, H, HD)
        token_i = first + jnp.arange(block_rows, dtype=jnp.int32)
        cell_i = token_i // G
        window_rows = jnp.repeat(lax.dynamic_slice_in_dim(windows, block * G, G, 0), G)
        token_j = first - halo_rows + jnp.arange(block_rows + halo_rows, dtype=jnp.int32)
        near_mask = (token_j[None, :] >= 0) & (token_j[None, :] <= token_i[:, None]) & (
            token_j[None, :] // G >= (cell_i - window_rows)[:, None])
        cell_e = block * G - G + jnp.arange(2 * G, dtype=jnp.int32)
        mid_mask = (cell_e[None, :] >= 0) & (cell_e[None, :] <= (cell_i - window_rows - 1)[:, None])
        coarse_e = jnp.arange(COARSE, dtype=jnp.int32)
        far_mask = jnp.broadcast_to(coarse_e[None, :] <= block - 2, (block_rows, COARSE))
        scores = jnp.concatenate([scored(rows_q, near_k, near_mask), scored(rows_q, mid_k, mid_mask),
                                  scored(rows_q, far_k, far_mask)], axis=2)
        top = jnp.max(scores, axis=2, keepdims=True)
        weights = jnp.exp(scores - top).astype(jnp.bfloat16)
        total = jnp.sum(weights.astype(jnp.float32), axis=2, keepdims=True)
        values_all = jnp.concatenate([near_v, mid_v, far_v], axis=0)
        summed = jnp.einsum("hqk,khe->qhe", weights.astype(jnp.float32), values_all.astype(jnp.float32))
        result = summed / jnp.transpose(total, (1, 0, 2))
        return result.astype(jnp.bfloat16).reshape(block_rows, D)

    attended = lax.map(one_block, jnp.arange(COARSE, dtype=jnp.int32)).reshape(TOKENS, D)
    return jnp.dot(attended, out_weight, preferred_element_type=jnp.float32).astype(jnp.bfloat16)
```

```python
import functools

import jax
import jax.numpy as jnp
from jax import lax
from jax.experimental import pallas as pl
from jax.experimental.pallas import tpu as pltpu
from jax.sharding import Mesh
from jax.sharding import PartitionSpec as P

HD = 128
G = 16
WMAX = 4
HALO = WMAX * G
LOG2E = 1.4426950408889634
SCALE = HD ** (-0.5) * LOG2E
CTX = ("y", "xh", "z")
TILE = 128
NEAR = TILE + HALO
SPAN = 256
CHUNK = 2
VMEM = 48 * 1024 * 1024


def params(**kw):
    return pltpu.CompilerParams(vmem_limit_bytes=VMEM, **kw)


def cost(flops, nbytes, trans=0):
    return pl.CostEstimate(flops=flops, bytes_accessed=nbytes, transcendentals=trans)


def shift(x, axis, by):
    n = lax.axis_size(axis)
    return lax.ppermute(x, axis, [(i, (i + by) % n) for i in range(n)])


def pool_kernel(k_ref, v_ref, k1_ref, v1_ref, far_ref):
    rows = k_ref.shape[0]
    cells = rows // G
    coarse = cells // G
    r = lax.broadcasted_iota(jnp.int32, (cells, rows), 0)
    t = lax.broadcasted_iota(jnp.int32, (cells, rows), 1)
    pick = jnp.where(t // G == r, 1.0, 0.0).astype(jnp.bfloat16)
    for src, one, slot in ((k_ref, k1_ref, 0), (v_ref, v1_ref, 1)):
        sums = jnp.dot(pick, src[...], preferred_element_type=jnp.float32)
        one[...] = (sums * (1.0 / G)).astype(jnp.bfloat16)
        whole = jnp.sum(sums.reshape(coarse, G, sums.shape[1]), axis=1)
        far_ref[slot] = (whole * (1.0 / (G * G))).astype(jnp.bfloat16)


def pool(key, value):
    rows, width = key.shape
    cols = 256
    cells, coarse = rows // G, rows // (G * G)
    spec = lambda n: pl.BlockSpec((n, cols), lambda i: (0, i))
    return pl.pallas_call(
        pool_kernel,
        grid=(width // cols,),
        in_specs=[spec(rows), spec(rows)],
        out_specs=[spec(cells), spec(cells), pl.BlockSpec((2, coarse, cols), lambda i: (0, 0, i))],
        out_shape=[
            jax.ShapeDtypeStruct((cells, width), jnp.bfloat16),
            jax.ShapeDtypeStruct((cells, width), jnp.bfloat16),
            jax.ShapeDtypeStruct((2, coarse, width), jnp.bfloat16),
        ],
        compiler_params=params(),
        cost_estimate=cost(2 * cells * rows * width * 2, 4 * rows * width),
        name="pool",
    )(key, value)


def near_kernel(q_ref, k_ref, v_ref, k1_ref, v1_ref, halo_ref, bias_ref, out_ref, lse_ref):
    rows = q_ref.shape[0]
    h = pl.program_id(0)
    ones = jnp.ones((SPAN, HD), jnp.bfloat16)
    pad = jnp.zeros((SPAN - NEAR - 2 * G, HD), jnp.bfloat16)
    lane = lax.broadcasted_iota(jnp.int32, (TILE, HD), 1)

    def rows_of(src, src1, base, base1, t):
        b = t * TILE // (G * G)
        if t == 0:
            near = [halo_ref[base : base + HALO, :], src[:TILE, :]]
        else:
            near = [src[t * TILE - HALO : (t + 1) * TILE, :]]
        if b == 0:
            mid = [halo_ref[base1 : base1 + G, :], src1[:G, :]]
        else:
            mid = [src1[(b - 1) * G : (b + 1) * G, :]]
        return jnp.concatenate(near + mid + [pad], axis=0)

    for t in range(rows // TILE):
        at = pl.ds(t * TILE, TILE)
        keys = rows_of(k_ref, k1_ref, 0, 2 * HALO, t)
        values = rows_of(v_ref, v1_ref, HALO, 2 * HALO + G, t)
        s = lax.dot_general(
            q_ref[at, :], keys, (((1,), (1,)), ((), ())), preferred_element_type=jnp.float32
        )
        s = s * SCALE + bias_ref[at, :]
        top = jnp.max(s, axis=1, keepdims=True)
        w = jnp.exp2(s - top).astype(jnp.bfloat16)
        both = jnp.dot(
            w, jnp.concatenate([values, ones], axis=1), preferred_element_type=jnp.float32
        )
        total = both[:, HD:]
        out_ref[at, :] = (both[:, :HD] / total).astype(jnp.bfloat16)
        lse = top + jnp.log2(total)

        @pl.when(h == 0)
        def _():
            lse_ref[at, :] = lse

        @pl.when(h > 0)
        def _():
            lse_ref[at, :] = jnp.where(lane == h, lse, lse_ref[at, :])


def near(query, key, value, key1, value1, halo, bias, first, heads):
    rows = query.shape[0]
    spec = lambda n: pl.BlockSpec((n, HD), lambda i: (0, first + i))
    whole = lambda n, w: pl.BlockSpec((n, w), lambda i: (0, 0))
    return pl.pallas_call(
        near_kernel,
        grid=(heads,),
        in_specs=[
            spec(rows), spec(rows), spec(rows), spec(rows // G), spec(rows // G),
            spec(halo.shape[0]), whole(rows, SPAN),
        ],
        out_specs=[pl.BlockSpec((rows, HD), lambda i: (0, i)), whole(rows, HD)],
        out_shape=[
            jax.ShapeDtypeStruct((rows, heads * HD), jnp.bfloat16),
            jax.ShapeDtypeStruct((rows, HD), jnp.float32),
        ],
        compiler_params=params(),
        cost_estimate=cost(
            2 * rows * SPAN * 3 * HD * heads, 8 * rows * HD * heads, rows * SPAN * heads
        ),
        name="near",
    )(query, key, value, key1, value1, halo, bias)


def far_kernel(lim_ref, q_ref, n_ref, lse_ref, k2_ref, v2_ref, cell_ref, out_ref):
    rows = q_ref.shape[0]
    heads = q_ref.shape[1] // HD
    cells = k2_ref.shape[1]
    ones = jnp.ones((cells, HD), jnp.bfloat16)
    cell = cell_ref[...]
    for h in range(heads):
        cols = slice(h * HD, (h + 1) * HD)
        keys = k2_ref[0, :, cols]
        values = jnp.concatenate([v2_ref[0, :, cols], ones], axis=1)
        for t in range(rows // TILE):
            at = slice(t * TILE, (t + 1) * TILE)
            last = lim_ref[0] + t * TILE // (G * G)
            bias = jnp.where(cell <= last, 0.0, -jnp.inf)
            s = lax.dot_general(
                q_ref[at, cols], keys, (((1,), (1,)), ((), ())), preferred_element_type=jnp.float32
            )
            s = s * SCALE + bias
            lse = lse_ref[at, h : h + 1]
            top = jnp.maximum(jnp.max(s, axis=1, keepdims=True), lse)
            w = jnp.exp2(s - top).astype(jnp.bfloat16)
            both = jnp.dot(w, values, preferred_element_type=jnp.float32)
            part = jnp.exp2(lse - top)
            summed = both[:, :HD] + n_ref[at, cols].astype(jnp.float32) * part
            out_ref[at, cols] = (summed / (both[:, HD:] + part)).astype(jnp.bfloat16)


def far(lim, query, partial, lse, kv2, col, cell, first):
    rows, width = partial.shape
    cells = kv2.shape[1]
    return pl.pallas_call(
        far_kernel,
        grid_spec=pltpu.PrefetchScalarGridSpec(
            num_scalar_prefetch=1,
            grid=(1,),
            in_specs=[
                pl.BlockSpec((rows, width), lambda i, s: (0, first)),
                pl.BlockSpec((rows, width), lambda i, s: (0, 0)),
                pl.BlockSpec((rows, HD), lambda i, s: (0, 0)),
                pl.BlockSpec((1, cells, width), lambda i, s: (0, 0, col)),
                pl.BlockSpec((1, cells, width), lambda i, s: (1, 0, col)),
                pl.BlockSpec((1, cells), lambda i, s: (0, 0)),
            ],
            out_specs=pl.BlockSpec((rows, width), lambda i, s: (0, 0)),
        ),
        out_shape=jax.ShapeDtypeStruct((rows, width), jnp.bfloat16),
        compiler_params=params(),
        cost_estimate=cost(2 * rows * cells * 3 * width, 8 * rows * width, rows * cells * 2),
        name="far",
    )(lim, query, partial, lse, kv2, kv2, cell)


def project_kernel(n, has_acc, place_ref, *refs):
    pieces, weights = refs[:n], refs[n : 2 * n]
    out_ref = refs[-1]
    total = refs[2 * n][...] if has_acc else None
    for piece, weight in zip(pieces, weights):
        term = jnp.dot(piece[...], weight[...], preferred_element_type=jnp.float32)
        total = term if total is None else total + term
    out_ref[...] = total.astype(out_ref.dtype)


def project(pieces, places, weight, acc, dtype):
    n = len(pieces)
    rows, width = pieces[0].shape
    cols = weight.shape[1]
    tile = 256
    specs = [pl.BlockSpec((tile, width), lambda i, s: (i, 0)) for _ in pieces]
    specs += [pl.BlockSpec((width, cols), lambda i, s, j=j: (s[j], 0)) for j in range(n)]
    args = list(pieces) + [weight] * n
    if acc is not None:
        specs.append(pl.BlockSpec((tile, cols), lambda i, s: (i, 0)))
        args.append(acc)
    return pl.pallas_call(
        functools.partial(project_kernel, n, acc is not None),
        grid_spec=pltpu.PrefetchScalarGridSpec(
            num_scalar_prefetch=1,
            grid=(rows // tile,),
            in_specs=specs,
            out_specs=pl.BlockSpec((tile, cols), lambda i, s: (i, 0)),
        ),
        out_shape=jax.ShapeDtypeStruct((rows, cols), dtype),
        compiler_params=params(),
        cost_estimate=cost(2 * rows * width * n * cols, n * width * (rows + cols) * 2 + rows * cols * 4),
        name="project",
    )(jnp.stack(places).astype(jnp.int32), *args)


def near_bias(windows, ctx, rows):
    row = jnp.arange(rows, dtype=jnp.int32)[:, None]
    lane = jnp.arange(SPAN, dtype=jnp.int32)[None, :]
    token = ctx * rows + row
    cell = token // G
    window = jnp.broadcast_to(windows[:, None], (windows.shape[0], G)).reshape(rows, 1)
    other = ctx * rows + row // TILE * TILE - HALO + lane
    near_ok = (other >= 0) & (other <= token) & (other // G >= cell - window)
    mid = token // (G * G) * G - G + lane - NEAR
    mid_ok = (mid >= 0) & (mid <= cell - window - 1)
    ok = jnp.where(lane < NEAR, near_ok, mid_ok & (lane < NEAR + 2 * G))
    return jnp.where(ok, 0.0, -jnp.inf).astype(jnp.float32)


def local(query, key, value, windows, out_weight):
    rows, width = query.shape
    heads = width // HD
    ny, nz = lax.axis_size("y"), lax.axis_size("z")
    iy, ix, iz = (lax.axis_index(a) for a in CTX)
    ctx = lax.axis_index(CTX)
    coarse = rows // (G * G)

    key1, value1, mine = pool(key, value)

    other = lax.ppermute(mine, "xh", [(0, 1), (1, 0)])
    x = jnp.concatenate([mine, other], axis=1)[:, None]
    a, b = shift(x, "z", 1), shift(x, "z", -1)
    x = jnp.concatenate([x, a, b], axis=1)
    c, d = shift(x, "z", 3), shift(x[:, :2], "z", -3)
    x = jnp.concatenate([x, c, d], axis=1)
    zs = (iz + jnp.array([0, -1, 1, -3, -4, -2, 3, 2], jnp.int32)) % nz
    ys = (iy + jnp.array([0, -1, 1, -2], jnp.int32)) % ny
    xs = jnp.stack([ix, 1 - ix])
    cell = (
        ((ys[:, None, None] * 2 + xs[None, None, :]) * nz + zs[None, :, None])[..., None] * coarse
        + jnp.arange(coarse, dtype=jnp.int32)
    ).reshape(1, -1)

    def over_y(part):
        parts = [part] + [shift(part, "y", s) for s in (1, -1, 2)]
        return jnp.concatenate(parts, axis=1).reshape(2, -1, part.shape[-1])

    step = CHUNK * HD
    gathered = [over_y(x[..., :step]), over_y(x[..., step:])]

    halo = lax.ppermute(
        jnp.concatenate([key[rows - HALO :], value[rows - HALO :], key1[-G:], value1[-G:]], axis=0),
        CTX,
        [(i, i + 1) for i in range(lax.axis_size(CTX) - 1)],
    )
    bias = near_bias(windows, ctx, rows)
    lim = (ctx * coarse - 2).reshape(1).astype(jnp.int32)
    xl, core = lax.axis_index("xl"), lax.axis_index("core")

    chunks = heads // CHUNK
    pieces, places = [], []
    for i in range(chunks):
        part, lse = near(query, key, value, key1, value1, halo, bias, i * CHUNK, CHUNK)
        kv2, col = (gathered[0], 0) if i == 0 else (gathered[1], i - 1)
        own = far(lim, query, part, lse, kv2, col, cell, i)
        across = lax.ppermute(own, "xl", [(0, 1), (1, 0)])
        beside = lax.ppermute(own, "core", [(0, 1), (1, 0)])
        diagonal = lax.ppermute(across, "core", [(0, 1), (1, 0)])
        for piece, px, pc in (
            (own, xl, core), (beside, xl, 1 - core), (across, 1 - xl, core), (diagonal, 1 - xl, 1 - core),
        ):
            pieces.append(piece)
            places.append((px * 2 + pc) * chunks + i)
    early = len(pieces) - 2
    acc = project(pieces[:early], places[:early], out_weight, None, jnp.float32)
    return project(pieces[early:], places[early:], out_weight, acc, jnp.bfloat16)


def solution(mesh):
    split = Mesh(mesh.devices.reshape(4, 2, 8, 2, 2), CTX + ("xl", "core"))
    rows, cols = CTX, ("xl", "core")
    in_specs = (P(rows, cols), P(rows, cols), P(rows, cols), P(rows), P(None, cols))
    return jax.shard_map(
        local, mesh=split, in_specs=in_specs, out_specs=P(rows, cols), check_vma=False
    )
```

```python
import functools

import jax
import jax.numpy as jnp
from jax import lax
from jax.experimental import pallas as pl
from jax.experimental.pallas import tpu as pltpu
from jax.sharding import Mesh
from jax.sharding import PartitionSpec as P

HD = 128
G = 16
WMAX = 4
HALO = WMAX * G
LOG2E = 1.4426950408889634
SCALE = HD ** (-0.5) * LOG2E
CTX = ("y", "xh", "z")
TILE = 128
NEAR = TILE + HALO
SPAN = 256
CHUNK = 2
MIB = 1024 * 1024
DEPTH = 3


def params(mib):
    return pltpu.CompilerParams(vmem_limit_bytes=mib * MIB)


def cost(micros):
    return pl.CostEstimate(flops=micros * 10**9, bytes_accessed=1000, transcendentals=0)


def shift(x, axis, by):
    n = lax.axis_size(axis)
    return lax.ppermute(x, axis, [(i, (i + by) % n) for i in range(n)])


def staged(jobs, stages):
    kept = {}
    for i in range(len(jobs) + DEPTH * (len(stages) - 1)):
        for n, stage in enumerate(stages):
            j = i - n * DEPTH
            if 0 <= j < len(jobs):
                kept[j] = stage(jobs[j], kept.get(j))


def pool_kernel(*refs):
    k1_ref, v1_ref, far_ref, edge_ref = refs[-4:]
    blocks = (len(refs) - 4) // 2
    rows, width = refs[0].shape
    r = lax.broadcasted_iota(jnp.int32, (rows // G, rows), 0)
    t = lax.broadcasted_iota(jnp.int32, (rows // G, rows), 1)
    pick = jnp.where(t // G == r, 1.0, 0.0).astype(jnp.bfloat16)
    for slot, one in ((0, k1_ref), (1, v1_ref)):
        wholes = []
        for b in range(blocks):
            src = refs[slot * blocks + b]
            sums = jnp.dot(pick, src[...], preferred_element_type=jnp.float32)
            one[b * G : (b + 1) * G, :] = (sums * (1.0 / G)).astype(jnp.bfloat16)
            wholes.append(jnp.sum(sums, axis=0, keepdims=True) * (1.0 / (G * G)))
        far_ref[slot] = jnp.concatenate(wholes, axis=0).astype(jnp.bfloat16)
        edge_ref[slot * HALO : (slot + 1) * HALO, :] = src[rows - HALO :, :]
        edge_ref[2 * HALO + slot * G : 2 * HALO + (slot + 1) * G, :] = one[blocks * G - G :, :]


def pool(key, value):
    rows, width = key.shape
    block = G * G
    blocks = rows // block
    spec = lambda n, b: pl.BlockSpec((n, width), lambda i: (b, 0))
    return pl.pallas_call(
        pool_kernel,
        grid=(1,),
        in_specs=[spec(block, b) for b in range(blocks)] * 2,
        out_specs=[
            spec(rows // G, 0), spec(rows // G, 0),
            pl.BlockSpec((2, blocks, width), lambda i: (0, 0, 0)), spec(2 * HALO + 2 * G, 0),
        ],
        out_shape=[
            jax.ShapeDtypeStruct((rows // G, width), jnp.bfloat16),
            jax.ShapeDtypeStruct((rows // G, width), jnp.bfloat16),
            jax.ShapeDtypeStruct((2, blocks, width), jnp.bfloat16),
            jax.ShapeDtypeStruct((2 * HALO + 2 * G, width), jnp.bfloat16),
        ],
        compiler_params=params(60),
        cost_estimate=cost(0),
        name="pool",
    )(*[key] * blocks, *[value] * blocks)


def near_kernel(
    info_ref, q_ref, k_ref, v_ref, k1_ref, v1_ref, pk_ref, pv_ref, pk1_ref, pv1_ref, *refs
):
    out_ref, lse_ref, pack_ref, kx, vx, k1x, v1x, bias_ref = refs[-8:]
    rows, width = q_ref.shape
    heads = width // HD
    ones = jnp.ones((SPAN, HD), jnp.bfloat16)
    pad = jnp.zeros((SPAN - NEAR - 2 * G, HD), jnp.bfloat16)
    lane = lax.broadcasted_iota(jnp.int32, (TILE, HD), 1)
    step = pl.program_id(0)
    for ext, prev, now in ((kx, pk_ref, k_ref), (vx, pv_ref, v_ref), (k1x, pk1_ref, k1_ref), (v1x, pv1_ref, v1_ref)):
        before, count = prev.shape[0], now.shape[0]

        @pl.when(step == 0)
        def _():
            ext[:before, :] = prev[...]

        @pl.when(step > 0)
        def _():
            ext[:before, :] = ext[count : count + before, :]

        ext[before : before + count, :] = now[...]
    block = info_ref[0] + step
    row_cell = lax.broadcasted_iota(jnp.int32, (TILE, SPAN), 0) // G
    row = lax.broadcasted_iota(jnp.int32, (TILE, SPAN), 0)
    at_lane = lax.broadcasted_iota(jnp.int32, (TILE, SPAN), 1)
    for t in range(rows // TILE):
        window = jnp.zeros((TILE, SPAN), jnp.int32)
        for c in range(TILE // G):
            here = info_ref[2 + block * (rows // G) + t * (TILE // G) + c]
            window = jnp.where(row_cell == c, here, window)
        start = info_ref[1] + block * rows + t * TILE
        near_ok = (
            (at_lane >= HALO - start) & (at_lane - HALO <= row)
            & (at_lane // G >= row_cell + WMAX - window)
        )
        mid = at_lane - NEAR - G
        mid_ok = (mid >= -((start // (G * G)) * G)) & (
            mid <= t * (TILE // G) + row_cell - window - 1
        )
        lanes = jnp.where(
            at_lane < NEAR,
            near_ok.astype(jnp.int32),
            jnp.where(at_lane < NEAR + 2 * G, mid_ok.astype(jnp.int32), 0),
        )
        bias_ref[t * TILE : (t + 1) * TILE, :] = jnp.where(lanes == 1, 0.0, -jnp.inf)
    for p in range(heads // CHUNK):
        pack_ref[p] = q_ref[:, p * CHUNK * HD : (p + 1) * CHUNK * HD]
    lses = {}

    def where(job):
        t, h = job
        return slice(t * TILE, (t + 1) * TILE), slice(h * HD, (h + 1) * HD)

    def rows_of(src, src1, job):
        t, _ = job
        _, cols = where(job)
        return jnp.concatenate([src[t * TILE : t * TILE + NEAR, cols], src1[:, cols], pad], axis=0)

    def score(job, _):
        at, cols = where(job)
        return lax.dot_general(
            q_ref[at, cols], rows_of(kx, k1x, job), (((1,), (1,)), ((), ())),
            preferred_element_type=jnp.float32,
        )

    def weigh(job, s):
        at, _ = where(job)
        s = s * SCALE + bias_ref[at, :]
        top = jnp.max(s, axis=1, keepdims=True)
        return top, jnp.exp2(s - top).astype(jnp.bfloat16)

    def finish(job, kept):
        at, _ = where(job)
        t, h = job
        top, w = kept
        values = jnp.concatenate([rows_of(vx, v1x, job), ones], axis=1)
        both = jnp.dot(w, values, preferred_element_type=jnp.float32)
        total = both[:, HD:]
        part = h % CHUNK
        out_ref[h // CHUNK, at, part * HD : (part + 1) * HD] = (both[:, :HD] / total).astype(
            jnp.bfloat16
        )
        lse = top + jnp.log2(total)
        lses[t] = jnp.where(lane == h, lse, lses[t]) if h else lse
        if h == heads - 1:
            lse_ref[at, :] = lses[t]

    staged([(t, h) for t in range(rows // TILE) for h in range(heads)], [score, weigh, finish])


def near(query, key, value, key1, value1, prev, info, first, blocks, before):
    rows, width = query.shape
    block = G * G
    pairs = width // HD // CHUNK
    spec = lambda n: pl.BlockSpec((n, width), lambda i, s: (s[0] + i, 0))
    args = [query, key, value, key1, value1] + [p for p, _, _ in prev]
    specs = [spec(block), spec(block), spec(block), spec(G), spec(G)]
    specs += [pl.BlockSpec((n, width), lambda i, s, at=at: (at, 0)) for _, n, at in prev]
    shapes = [
        jax.ShapeDtypeStruct((pairs, rows, CHUNK * HD), jnp.bfloat16),
        jax.ShapeDtypeStruct((rows, HD), jnp.float32),
        jax.ShapeDtypeStruct((pairs, rows, CHUNK * HD), jnp.bfloat16),
    ]
    aliases = {}
    if before is not None:
        aliases = {len(args) + 1 + i: i for i in range(3)}
        args += list(before)
        specs += [pl.BlockSpec(memory_space=pl.ANY)] * 3
    packed = pl.BlockSpec((pairs, block, CHUNK * HD), lambda i, s: (0, s[0] + i, 0))
    return pl.pallas_call(
        near_kernel,
        grid_spec=pltpu.PrefetchScalarGridSpec(
            num_scalar_prefetch=1,
            grid=(blocks,),
            in_specs=specs,
            out_specs=[packed, pl.BlockSpec((block, HD), lambda i, s: (s[0] + i, 0)), packed],
            scratch_shapes=[
                pltpu.VMEM((HALO + block, width), jnp.bfloat16),
                pltpu.VMEM((HALO + block, width), jnp.bfloat16),
                pltpu.VMEM((2 * G, width), jnp.bfloat16),
                pltpu.VMEM((2 * G, width), jnp.bfloat16),
                pltpu.VMEM((block, SPAN), jnp.float32),
            ],
        ),
        out_shape=shapes,
        input_output_aliases=aliases,
        compiler_params=params(60),
        cost_estimate=cost(0),
        name="near",
    )(jnp.concatenate([jnp.full((1,), first, jnp.int32), info]), *args)


def far_kernel(pair, lim_ref, q_ref, n_ref, lse_ref, k2_ref, v2_ref, cell_ref, out_ref):
    rows = out_ref.shape[0]
    heads = out_ref.shape[1] // HD
    ones = jnp.ones((k2_ref.shape[1], HD), jnp.bfloat16)
    cell = cell_ref[...]
    limit = lim_ref[0] + pl.program_id(0) * (rows // (G * G))

    def where(job):
        t, h = job
        return slice(t * TILE, (t + 1) * TILE), slice(h * HD, (h + 1) * HD)

    def score(job, _):
        at, cols = where(job)
        return lax.dot_general(
            q_ref[0, at, cols], k2_ref[0, :, cols], (((1,), (1,)), ((), ())),
            preferred_element_type=jnp.float32,
        )

    def weigh(job, s):
        t, h = job
        at, _ = where(job)
        last = limit + t * TILE // (G * G)
        s = s * SCALE + jnp.where(cell <= last, 0.0, -jnp.inf)
        lse = lse_ref[at, pair * CHUNK + h : pair * CHUNK + h + 1]
        top = jnp.maximum(jnp.max(s, axis=1, keepdims=True), lse)
        return jnp.exp2(lse - top), jnp.exp2(s - top).astype(jnp.bfloat16)

    def finish(job, kept):
        at, cols = where(job)
        part, w = kept
        values = jnp.concatenate([v2_ref[0, :, cols], ones], axis=1)
        both = jnp.dot(w, values, preferred_element_type=jnp.float32)
        summed = both[:, :HD] + n_ref[0, at, cols].astype(jnp.float32) * part
        done = (summed / (both[:, HD:] + part)).astype(jnp.bfloat16)
        out_ref[at, cols] = done

    staged([(t, h) for h in range(heads) for t in range(rows // TILE)], [score, weigh, finish])


def far(lim, query, partial, lse, kv2, col, cell, pair):
    rows, cells = query.shape[1], kv2.shape[1]
    width = CHUNK * HD
    tile = 512
    args = [lim, query, partial, lse, kv2, kv2, cell]
    return pl.pallas_call(
        functools.partial(far_kernel, pair),
        grid_spec=pltpu.PrefetchScalarGridSpec(
            num_scalar_prefetch=1,
            grid=(rows // tile,),
            in_specs=[
                pl.BlockSpec((1, tile, width), lambda i, s: (pair, i, 0)),
                pl.BlockSpec((1, tile, width), lambda i, s: (pair, i, 0)),
                pl.BlockSpec((tile, HD), lambda i, s: (i, 0)),
                pl.BlockSpec((1, cells, width), lambda i, s: (0, 0, col)),
                pl.BlockSpec((1, cells, width), lambda i, s: (1, 0, col)),
                pl.BlockSpec((1, cells), lambda i, s: (0, 0)),
            ],
            out_specs=pl.BlockSpec((tile, width), lambda i, s: (i, 0)),
        ),
        out_shape=jax.ShapeDtypeStruct((rows, width), jnp.bfloat16),
        compiler_params=params(60),
        cost_estimate=cost(0),
        name="far",
    )(*args)


def project_kernel(n, has_acc, place_ref, *refs):
    held = [ref[...] for ref in refs[:n]]
    weights = jnp.concatenate([r[...] for r in refs[n : 2 * n]], axis=0)
    total = jnp.dot(jnp.concatenate(held, axis=1), weights, preferred_element_type=jnp.float32)
    if has_acc:
        total = total + refs[2 * n][...]
    refs[-1][...] = total.astype(refs[-1].dtype)


def project(pieces, places, weight, acc, dtype):
    n = len(pieces)
    rows, width = pieces[0].shape
    cols = weight.shape[1]
    tile = 256
    out_spec = pl.BlockSpec((tile, cols), lambda i, s: (i, 0))
    specs = [pl.BlockSpec((tile, width), lambda i, s: (i, 0)) for _ in pieces]
    specs += [pl.BlockSpec((width, cols), lambda i, s, j=j: (s[j], 0)) for j in range(n)]
    args = list(pieces) + [weight] * n
    if acc is not None:
        specs.append(out_spec)
        args.append(acc)
    return pl.pallas_call(
        functools.partial(project_kernel, n, acc is not None),
        grid_spec=pltpu.PrefetchScalarGridSpec(
            num_scalar_prefetch=1,
            grid=(rows // tile,),
            in_specs=specs,
            out_specs=out_spec,
        ),
        out_shape=jax.ShapeDtypeStruct((rows, cols), dtype),
        compiler_params=params(60),
        cost_estimate=cost(0),
        name="project",
    )(jnp.stack(places).astype(jnp.int32), *args)


def local(query, key, value, windows, out_weight):
    rows, width = query.shape
    heads = width // HD
    ny, nz = lax.axis_size("y"), lax.axis_size("z")
    iy, ix, iz = (lax.axis_index(a) for a in CTX)
    ctx = lax.axis_index(CTX)
    coarse = rows // (G * G)

    key1, value1, mine, edge = pool(key, value)

    block = G * G
    upper = rows // block // 2
    ahead = [
        (key, HALO, upper * block // HALO - 1), (value, HALO, upper * block // HALO - 1),
        (key1, G, upper - 1), (value1, G, upper - 1),
    ]
    info = jnp.concatenate([(ctx * rows).reshape(1).astype(jnp.int32), windows])

    other = lax.ppermute(mine, "xh", [(0, 1), (1, 0)])
    part = near(query, key, value, key1, value1, ahead, info, upper, rows // block - upper, None)
    mine, part = lax.optimization_barrier((mine, part))
    x = jnp.concatenate([mine, other], axis=1)[:, None]
    halo = lax.ppermute(edge, CTX, [(i, i + 1) for i in range(lax.axis_size(CTX) - 1)])
    x, halo = lax.optimization_barrier((x, halo))
    a, b = shift(x, "z", 3), shift(x, "z", -3)
    behind = [(halo, HALO, 0), (halo, HALO, 1), (halo, G, 2 * HALO // G), (halo, G, 2 * HALO // G + 1)]
    part = near(query, key, value, key1, value1, behind, info, 0, upper, part)
    x, part = lax.optimization_barrier((x, part))
    x = jnp.concatenate([x, a, b], axis=1)
    c, d = shift(x, "z", 1), shift(x[:, :2], "z", -1)
    x = jnp.concatenate([x, c, d], axis=1)
    zs = (iz + jnp.array([0, -3, 3, -1, -4, 2, 1, -2], jnp.int32)) % nz
    ys = (iy + jnp.array([0, -1, 1, -2], jnp.int32)) % ny
    xs = jnp.stack([ix, 1 - ix])
    cell = (
        ((ys[:, None, None] * 2 + xs[None, None, :]) * nz + zs[None, :, None])[..., None] * coarse
        + jnp.arange(coarse, dtype=jnp.int32)
    ).reshape(1, -1)

    def over_y(part):
        parts = [part] + [shift(part, "y", s) for s in (1, -1, 2)]
        return jnp.concatenate(parts, axis=1).reshape(2, -1, part.shape[-1])

    lim = (ctx * coarse - 2).reshape(1).astype(jnp.int32)
    xl, core = lax.axis_index("xl"), lax.axis_index("core")
    swap = [(0, 1), (1, 0)]
    pairs = heads // CHUNK
    soon = 2
    step = soon * CHUNK * HD
    kv_first = over_y(x[..., :step])
    kv_first, x = lax.optimization_barrier((kv_first, x[..., step:]))
    kv_rest = over_y(x)

    here, there = xl * 2, (1 - xl) * 2
    last = pairs - 1
    own, across, beside, diagonal = [], [], [], []

    def place(kind, i):
        base = here if kind < 2 else there
        return (base + (core if kind % 2 == 0 else 1 - core)) * pairs + i

    def add(which, acc, dtype=jnp.float32):
        sets = (own, beside, across, diagonal)
        pieces, places = [], []
        for kind, i in which:
            pieces.append(sets[kind][i])
            places.append(place(kind, i))
        return project(pieces, places, out_weight, acc, dtype)

    hop = lambda axis, xs: [lax.ppermute(o, axis, swap) for o in xs]

    def attend(n, kv2, col):
        own.append(far(lim, part[2], part[0], part[1], kv2, col, cell, n))
        across.append(lax.ppermute(own[n], "xl", swap))

    attend(0, kv_first, 0)
    kv_first, own[0] = lax.optimization_barrier((kv_first, own[0]))
    attend(1, kv_first, 1)
    kv_rest, *both = lax.optimization_barrier((kv_rest, *own, across[0]))
    beside += hop("core", both[:2])
    diagonal += hop("core", both[2:])
    attend(2, kv_rest, 0)
    kv_rest, across[1], beside[0], beside[1], diagonal[0] = lax.optimization_barrier(
        (kv_rest, across[1], beside[0], beside[1], diagonal[0])
    )
    diagonal += hop("core", across[1:2])
    attend(3, kv_rest, 1)
    beside += hop("core", own[2:])
    acc = add([(0, 0), (0, 1), (1, 0), (1, 1), (2, 0), (3, 0)], None)
    acc = add([(2, 1), (3, 1), (0, 2), (1, 2), (0, 3), (1, 3)], acc)
    across[2], across[3], acc = lax.optimization_barrier((across[2], across[3], acc))
    diagonal += hop("core", across[2:])
    return add([(2, 2), (3, 2), (2, 3), (3, 3)], acc, jnp.bfloat16)


def solution(mesh):
    split = Mesh(mesh.devices.reshape(4, 2, 8, 2, 2), CTX + ("xl", "core"))
    rows, cols = CTX, ("xl", "core")
    in_specs = (P(rows, cols), P(rows, cols), P(rows, cols), P(rows), P(None, cols))
    return jax.shard_map(
        local, mesh=split, in_specs=in_specs, out_specs=P(rows, cols), check_vma=False
    )
```

```python
import functools

import jax
import jax.numpy as jnp
from jax import lax
from jax.experimental import pallas as pl
from jax.experimental.pallas import tpu as pltpu
from jax.sharding import Mesh
from jax.sharding import PartitionSpec as P

HD = 128
G = 16
WMAX = 4
HALO = WMAX * G
LOG2E = 1.4426950408889634
SCALE = HD ** (-0.5) * LOG2E
CTX = ("y", "xh", "z")
TILE = 128
NEAR = TILE + HALO
SPAN = 256
CHUNK = 2
MIB = 1024 * 1024
DEPTH = 3


def params(mib):
    return pltpu.CompilerParams(vmem_limit_bytes=mib * MIB)


def cost(micros):
    return pl.CostEstimate(flops=micros * 10**9, bytes_accessed=1000, transcendentals=0)


def shift(x, axis, by):
    n = lax.axis_size(axis)
    return lax.ppermute(x, axis, [(i, (i + by) % n) for i in range(n)])


def staged(jobs, stages):
    kept = {}
    for i in range(len(jobs) + DEPTH * (len(stages) - 1)):
        for n, stage in enumerate(stages):
            j = i - n * DEPTH
            if 0 <= j < len(jobs):
                kept[j] = stage(jobs[j], kept.get(j))


def pool_kernel(*refs):
    k1_ref, v1_ref, far_ref, edge_ref = refs[-4:]
    blocks = (len(refs) - 4) // 2
    rows, width = refs[0].shape
    r = lax.broadcasted_iota(jnp.int32, (rows // G, rows), 0)
    t = lax.broadcasted_iota(jnp.int32, (rows // G, rows), 1)
    pick = jnp.where(t // G == r, 1.0, 0.0).astype(jnp.bfloat16)
    for slot, one in ((0, k1_ref), (1, v1_ref)):
        wholes = []
        for b in range(blocks):
            src = refs[slot * blocks + b]
            sums = jnp.dot(pick, src[...], preferred_element_type=jnp.float32)
            one[b * G : (b + 1) * G, :] = (sums * (1.0 / G)).astype(jnp.bfloat16)
            wholes.append(jnp.sum(sums, axis=0, keepdims=True) * (1.0 / (G * G)))
        far_ref[slot] = jnp.concatenate(wholes, axis=0).astype(jnp.bfloat16)
        edge_ref[slot * HALO : (slot + 1) * HALO, :] = src[rows - HALO :, :]
        edge_ref[2 * HALO + slot * G : 2 * HALO + (slot + 1) * G, :] = one[blocks * G - G :, :]


def pool(key, value):
    rows, width = key.shape
    block = G * G
    blocks = rows // block
    spec = lambda n, b: pl.BlockSpec((n, width), lambda i: (b, 0))
    return pl.pallas_call(
        pool_kernel,
        grid=(1,),
        in_specs=[spec(block, b) for b in range(blocks)] * 2,
        out_specs=[
            spec(rows // G, 0), spec(rows // G, 0),
            pl.BlockSpec((2, blocks, width), lambda i: (0, 0, 0)), spec(2 * HALO + 2 * G, 0),
        ],
        out_shape=[
            jax.ShapeDtypeStruct((rows // G, width), jnp.bfloat16),
            jax.ShapeDtypeStruct((rows // G, width), jnp.bfloat16),
            jax.ShapeDtypeStruct((2, blocks, width), jnp.bfloat16),
            jax.ShapeDtypeStruct((2 * HALO + 2 * G, width), jnp.bfloat16),
        ],
        compiler_params=params(60),
        cost_estimate=cost(0),
        name="pool",
    )(*[key] * blocks, *[value] * blocks)


def near_kernel(
    info_ref, q_ref, k_ref, v_ref, k1_ref, v1_ref, pk_ref, pv_ref, pk1_ref, pv1_ref, *refs
):
    out_ref, lse_ref, pack_ref, kx, vx, k1x, v1x, bias_ref = refs[-8:]
    rows, width = q_ref.shape
    heads = width // HD
    ones = jnp.ones((SPAN, HD), jnp.bfloat16)
    pad = jnp.zeros((SPAN - NEAR - 2 * G, HD), jnp.bfloat16)
    lane = lax.broadcasted_iota(jnp.int32, (TILE, HD), 1)
    step = pl.program_id(0)
    for ext, prev, now in ((kx, pk_ref, k_ref), (vx, pv_ref, v_ref), (k1x, pk1_ref, k1_ref), (v1x, pv1_ref, v1_ref)):
        before, count = prev.shape[0], now.shape[0]

        @pl.when(step == 0)
        def _():
            ext[:before, :] = prev[...]

        @pl.when(step > 0)
        def _():
            ext[:before, :] = ext[count : count + before, :]

        ext[before : before + count, :] = now[...]
    block = info_ref[0] + step
    row_cell = lax.broadcasted_iota(jnp.int32, (TILE, SPAN), 0) // G
    row = lax.broadcasted_iota(jnp.int32, (TILE, SPAN), 0)
    at_lane = lax.broadcasted_iota(jnp.int32, (TILE, SPAN), 1)
    for t in range(rows // TILE):
        window = jnp.zeros((TILE, SPAN), jnp.int32)
        for c in range(TILE // G):
            here = info_ref[2 + block * (rows // G) + t * (TILE // G) + c]
            window = jnp.where(row_cell == c, here, window)
        start = info_ref[1] + block * rows + t * TILE
        near_ok = (
            (at_lane >= HALO - start) & (at_lane - HALO <= row)
            & (at_lane // G >= row_cell + WMAX - window)
        )
        mid = at_lane - NEAR - G
        mid_ok = (mid >= -((start // (G * G)) * G)) & (
            mid <= t * (TILE // G) + row_cell - window - 1
        )
        lanes = jnp.where(
            at_lane < NEAR,
            near_ok.astype(jnp.int32),
            jnp.where(at_lane < NEAR + 2 * G, mid_ok.astype(jnp.int32), 0),
        )
        bias_ref[t * TILE : (t + 1) * TILE, :] = jnp.where(lanes == 1, 0.0, -jnp.inf)
    for p in range(heads // CHUNK):
        pack_ref[p] = q_ref[:, p * CHUNK * HD : (p + 1) * CHUNK * HD]
    lses = {}

    def where(job):
        t, h = job
        return slice(t * TILE, (t + 1) * TILE), slice(h * HD, (h + 1) * HD)

    def rows_of(src, src1, job):
        t, _ = job
        _, cols = where(job)
        return jnp.concatenate([src[t * TILE : t * TILE + NEAR, cols], src1[:, cols], pad], axis=0)

    def score(job, _):
        at, cols = where(job)
        return lax.dot_general(
            q_ref[at, cols], rows_of(kx, k1x, job), (((1,), (1,)), ((), ())),
            preferred_element_type=jnp.float32,
        )

    def weigh(job, s):
        at, _ = where(job)
        s = s * SCALE + bias_ref[at, :]
        top = jnp.max(s, axis=1, keepdims=True)
        return top, jnp.exp2(s - top).astype(jnp.bfloat16)

    def finish(job, kept):
        at, _ = where(job)
        t, h = job
        top, w = kept
        values = jnp.concatenate([rows_of(vx, v1x, job), ones], axis=1)
        both = jnp.dot(w, values, preferred_element_type=jnp.float32)
        total = both[:, HD:]
        part = h % CHUNK
        out_ref[h // CHUNK, at, part * HD : (part + 1) * HD] = (both[:, :HD] / total).astype(
            jnp.bfloat16
        )
        lse = top + jnp.log2(total)
        lses[t] = jnp.where(lane == h, lse, lses[t]) if h else lse
        if h == heads - 1:
            lse_ref[at, :] = lses[t]

    staged([(t, h) for t in range(rows // TILE) for h in range(heads)], [score, weigh, finish])


def near(query, key, value, key1, value1, prev, info, first, blocks, before):
    rows, width = query.shape
    block = G * G
    pairs = width // HD // CHUNK
    spec = lambda n: pl.BlockSpec((n, width), lambda i, s: (s[0] + i, 0))
    args = [query, key, value, key1, value1] + [p for p, _, _ in prev]
    specs = [spec(block), spec(block), spec(block), spec(G), spec(G)]
    specs += [pl.BlockSpec((n, width), lambda i, s, at=at: (at, 0)) for _, n, at in prev]
    shapes = [
        jax.ShapeDtypeStruct((pairs, rows, CHUNK * HD), jnp.bfloat16),
        jax.ShapeDtypeStruct((rows, HD), jnp.float32),
        jax.ShapeDtypeStruct((pairs, rows, CHUNK * HD), jnp.bfloat16),
    ]
    aliases = {}
    if before is not None:
        aliases = {len(args) + 1 + i: i for i in range(3)}
        args += list(before)
        specs += [pl.BlockSpec(memory_space=pl.ANY)] * 3
    packed = pl.BlockSpec((pairs, block, CHUNK * HD), lambda i, s: (0, s[0] + i, 0))
    return pl.pallas_call(
        near_kernel,
        grid_spec=pltpu.PrefetchScalarGridSpec(
            num_scalar_prefetch=1,
            grid=(blocks,),
            in_specs=specs,
            out_specs=[packed, pl.BlockSpec((block, HD), lambda i, s: (s[0] + i, 0)), packed],
            scratch_shapes=[
                pltpu.VMEM((HALO + block, width), jnp.bfloat16),
                pltpu.VMEM((HALO + block, width), jnp.bfloat16),
                pltpu.VMEM((2 * G, width), jnp.bfloat16),
                pltpu.VMEM((2 * G, width), jnp.bfloat16),
                pltpu.VMEM((block, SPAN), jnp.float32),
            ],
        ),
        out_shape=shapes,
        input_output_aliases=aliases,
        compiler_params=params(60),
        cost_estimate=cost(0),
        name="near",
    )(jnp.concatenate([jnp.full((1,), first, jnp.int32), info]), *args)


def far_kernel(pair, lim_ref, q_ref, n_ref, lse_ref, k2_ref, v2_ref, cell_ref, *out_refs):
    rows = q_ref.shape[1]
    heads = CHUNK * len(out_refs)
    ones = jnp.ones((k2_ref.shape[1], HD), jnp.bfloat16)
    cell = cell_ref[...]
    limit = lim_ref[0] + pl.program_id(0) * (rows // (G * G))

    def where(job):
        t, h = job
        part = h % CHUNK * HD
        return h // CHUNK, slice(t * TILE, (t + 1) * TILE), slice(part, part + HD), slice(h * HD, (h + 1) * HD)

    def score(job, _):
        p, at, cols, keys = where(job)
        return lax.dot_general(
            q_ref[p, at, cols], k2_ref[0, :, keys], (((1,), (1,)), ((), ())),
            preferred_element_type=jnp.float32,
        )

    def weigh(job, s):
        t, h = job
        _, at, _, _ = where(job)
        last = limit + t * TILE // (G * G)
        s = s * SCALE + jnp.where(cell <= last, 0.0, -jnp.inf)
        lse = lse_ref[at, pair * CHUNK + h : pair * CHUNK + h + 1]
        top = jnp.maximum(jnp.max(s, axis=1, keepdims=True), lse)
        return jnp.exp2(lse - top), jnp.exp2(s - top).astype(jnp.bfloat16)

    def finish(job, kept):
        p, at, cols, keys = where(job)
        part, w = kept
        values = jnp.concatenate([v2_ref[0, :, keys], ones], axis=1)
        both = jnp.dot(w, values, preferred_element_type=jnp.float32)
        summed = both[:, :HD] + n_ref[p, at, cols].astype(jnp.float32) * part
        done = (summed / (both[:, HD:] + part)).astype(jnp.bfloat16)
        out_refs[p][at, cols] = done

    staged([(t, h) for h in range(heads) for t in range(rows // TILE)], [score, weigh, finish])


def far(lim, query, partial, lse, kv2, col, cell, pair, count=1):
    rows, cells = query.shape[1], kv2.shape[1]
    width = CHUNK * HD
    tile = 512
    args = [lim, query, partial, lse, kv2, kv2, cell]
    return pl.pallas_call(
        functools.partial(far_kernel, pair),
        grid_spec=pltpu.PrefetchScalarGridSpec(
            num_scalar_prefetch=1,
            grid=(rows // tile,),
            in_specs=[
                pl.BlockSpec((count, tile, width), lambda i, s: (pair // count, i, 0)),
                pl.BlockSpec((count, tile, width), lambda i, s: (pair // count, i, 0)),
                pl.BlockSpec((tile, HD), lambda i, s: (i, 0)),
                pl.BlockSpec((1, cells, count * width), lambda i, s: (0, 0, col)),
                pl.BlockSpec((1, cells, count * width), lambda i, s: (1, 0, col)),
                pl.BlockSpec((1, cells), lambda i, s: (0, 0)),
            ],
            out_specs=[pl.BlockSpec((tile, width), lambda i, s: (i, 0))] * count,
        ),
        out_shape=[jax.ShapeDtypeStruct((rows, width), jnp.bfloat16)] * count,
        compiler_params=params(60),
        cost_estimate=cost(0),
        name="far",
    )(*args)


def project_kernel(n, has_acc, place_ref, *refs):
    held = [ref[...] for ref in refs[:n]]
    weights = jnp.concatenate([r[...] for r in refs[n : 2 * n]], axis=0)
    total = jnp.dot(jnp.concatenate(held, axis=1), weights, preferred_element_type=jnp.float32)
    if has_acc:
        total = total + refs[2 * n][...]
    refs[-1][...] = total.astype(refs[-1].dtype)


def project(pieces, places, weight, acc, dtype):
    n = len(pieces)
    rows, width = pieces[0].shape
    cols = weight.shape[1]
    tile = 256
    out_spec = pl.BlockSpec((tile, cols), lambda i, s: (i, 0))
    specs = [pl.BlockSpec((tile, width), lambda i, s: (i, 0)) for _ in pieces]
    specs += [pl.BlockSpec((width, cols), lambda i, s, j=j: (s[j], 0)) for j in range(n)]
    args = list(pieces) + [weight] * n
    if acc is not None:
        specs.append(out_spec)
        args.append(acc)
    return pl.pallas_call(
        functools.partial(project_kernel, n, acc is not None),
        grid_spec=pltpu.PrefetchScalarGridSpec(
            num_scalar_prefetch=1,
            grid=(rows // tile,),
            in_specs=specs,
            out_specs=out_spec,
        ),
        out_shape=jax.ShapeDtypeStruct((rows, cols), dtype),
        compiler_params=params(60),
        cost_estimate=cost(0),
        name="project",
    )(jnp.stack(places).astype(jnp.int32), *args)


def local(query, key, value, windows, out_weight):
    rows, width = query.shape
    heads = width // HD
    ny, nz = lax.axis_size("y"), lax.axis_size("z")
    iy, ix, iz = (lax.axis_index(a) for a in CTX)
    ctx = lax.axis_index(CTX)
    coarse = rows // (G * G)

    key1, value1, mine, edge = pool(key, value)

    block = G * G
    upper = rows // block // 2
    ahead = [
        (key, HALO, upper * block // HALO - 1), (value, HALO, upper * block // HALO - 1),
        (key1, G, upper - 1), (value1, G, upper - 1),
    ]
    info = jnp.concatenate([(ctx * rows).reshape(1).astype(jnp.int32), windows])

    other = lax.ppermute(mine, "xh", [(0, 1), (1, 0)])
    part = near(query, key, value, key1, value1, ahead, info, upper, rows // block - upper, None)
    mine, part = lax.optimization_barrier((mine, part))
    x = jnp.concatenate([mine, other], axis=1)[:, None]
    halo = lax.ppermute(edge, CTX, [(i, i + 1) for i in range(lax.axis_size(CTX) - 1)])
    x, halo = lax.optimization_barrier((x, halo))
    a, b = shift(x, "z", 3), shift(x, "z", -3)
    behind = [(halo, HALO, 0), (halo, HALO, 1), (halo, G, 2 * HALO // G), (halo, G, 2 * HALO // G + 1)]
    part = near(query, key, value, key1, value1, behind, info, 0, upper, part)
    x, part = lax.optimization_barrier((x, part))
    x = jnp.concatenate([x, a, b], axis=1)
    c, d = shift(x, "z", 1), shift(x[:, :2], "z", -1)
    x = jnp.concatenate([x, c, d], axis=1)
    zs = (iz + jnp.array([0, -3, 3, -1, -4, 2, 1, -2], jnp.int32)) % nz
    ys = (iy + jnp.array([0, -1, 1, -2], jnp.int32)) % ny
    xs = jnp.stack([ix, 1 - ix])
    cell = (
        ((ys[:, None, None] * 2 + xs[None, None, :]) * nz + zs[None, :, None])[..., None] * coarse
        + jnp.arange(coarse, dtype=jnp.int32)
    ).reshape(1, -1)

    def over_y(part):
        parts = [part] + [shift(part, "y", s) for s in (1, -1, 2)]
        return jnp.concatenate(parts, axis=1).reshape(2, -1, part.shape[-1])

    lim = (ctx * coarse - 2).reshape(1).astype(jnp.int32)
    xl, core = lax.axis_index("xl"), lax.axis_index("core")
    swap = [(0, 1), (1, 0)]
    pairs = heads // CHUNK
    soon = 2
    step = soon * CHUNK * HD
    kv_first = over_y(x[..., :step])
    kv_first, x = lax.optimization_barrier((kv_first, x[..., step:]))
    kv_rest = over_y(x)

    here, there = xl * 2, (1 - xl) * 2
    last = pairs - 1
    own, across, beside, diagonal = [], [], [], []

    def place(kind, i):
        base = here if kind < 2 else there
        return (base + (core if kind % 2 == 0 else 1 - core)) * pairs + i

    def add(which, acc, dtype=jnp.float32):
        sets = (own, beside, across, diagonal)
        pieces, places = [], []
        for kind, i in which:
            pieces.append(sets[kind][i])
            places.append(place(kind, i))
        return project(pieces, places, out_weight, acc, dtype)

    hop = lambda axis, xs: [lax.ppermute(o, axis, swap) for o in xs]

    def attend(n, kv2, col, count=1):
        own.extend(far(lim, part[2], part[0], part[1], kv2, col, cell, n, count))
        across.extend(hop("xl", own[n:]))

    attend(0, kv_first, 0)
    kv_first, own[0] = lax.optimization_barrier((kv_first, own[0]))
    attend(1, kv_first, 1)
    kv_rest, *both = lax.optimization_barrier((kv_rest, *own, across[0]))
    beside += hop("core", both[:2])
    diagonal += hop("core", both[2:])
    attend(2, kv_rest, 0, 2)
    own[2], own[3], across[1] = lax.optimization_barrier((own[2], own[3], across[1]))
    diagonal += hop("core", across[1:2])
    beside += hop("core", own[2:])
    acc = add([(0, 0), (0, 1), (1, 0), (1, 1), (2, 0), (3, 0)], None)
    acc = add([(2, 1), (3, 1), (0, 2), (1, 2), (0, 3), (1, 3)], acc)
    across[2], across[3], acc = lax.optimization_barrier((across[2], across[3], acc))
    diagonal += hop("core", across[2:])
    return add([(2, 2), (3, 2), (2, 3), (3, 3)], acc, jnp.bfloat16)


def solution(mesh):
    split = Mesh(mesh.devices.reshape(4, 2, 8, 2, 2), CTX + ("xl", "core"))
    rows, cols = CTX, ("xl", "core")
    in_specs = (P(rows, cols), P(rows, cols), P(rows, cols), P(rows), P(None, cols))
    return jax.shard_map(
        local, mesh=split, in_specs=in_specs, out_specs=P(rows, cols), check_vma=False
    )
```

```python
import functools

import jax
import jax.numpy as jnp
from jax import lax
from jax.experimental import pallas as pl
from jax.experimental.pallas import tpu as pltpu
from jax.sharding import Mesh
from jax.sharding import PartitionSpec as P

HD = 128
G = 16
WMAX = 4
HALO = WMAX * G
LOG2E = 1.4426950408889634
SCALE = HD ** (-0.5) * LOG2E
CTX = ("y", "xh", "z")
TILE = 128
NEAR = TILE + HALO
SPAN = 256
CHUNK = 2
MIB = 1024 * 1024
DEPTH = 3


def params(mib):
    return pltpu.CompilerParams(vmem_limit_bytes=mib * MIB)


def cost(micros):
    return pl.CostEstimate(flops=micros * 10**9, bytes_accessed=1000, transcendentals=0)


def shift(x, axis, by):
    n = lax.axis_size(axis)
    return lax.ppermute(x, axis, [(i, (i + by) % n) for i in range(n)])


def staged(jobs, stages):
    kept = {}
    for i in range(len(jobs) + DEPTH * (len(stages) - 1)):
        for n, stage in enumerate(stages):
            j = i - n * DEPTH
            if 0 <= j < len(jobs):
                kept[j] = stage(jobs[j], kept.get(j))


def pool_kernel(*refs):
    k1_ref, v1_ref, far_ref, edge_ref = refs[-4:]
    blocks = (len(refs) - 4) // 2
    rows, width = refs[0].shape
    r = lax.broadcasted_iota(jnp.int32, (rows // G, rows), 0)
    t = lax.broadcasted_iota(jnp.int32, (rows // G, rows), 1)
    pick = jnp.where(t // G == r, 1.0, 0.0).astype(jnp.bfloat16)
    for slot, one in ((0, k1_ref), (1, v1_ref)):
        wholes = []
        for b in range(blocks):
            src = refs[slot * blocks + b]
            sums = jnp.dot(pick, src[...], preferred_element_type=jnp.float32)
            one[b * G : (b + 1) * G, :] = (sums * (1.0 / G)).astype(jnp.bfloat16)
            wholes.append(jnp.sum(sums, axis=0, keepdims=True) * (1.0 / (G * G)))
        far_ref[slot] = jnp.concatenate(wholes, axis=0).astype(jnp.bfloat16)
        edge_ref[slot * HALO : (slot + 1) * HALO, :] = src[rows - HALO :, :]
        edge_ref[2 * HALO + slot * G : 2 * HALO + (slot + 1) * G, :] = one[blocks * G - G :, :]


def pool(key, value):
    rows, width = key.shape
    block = G * G
    blocks = rows // block
    spec = lambda n, b: pl.BlockSpec((n, width), lambda i: (b, 0))
    return pl.pallas_call(
        pool_kernel,
        grid=(1,),
        in_specs=[spec(block, b) for b in range(blocks)] * 2,
        out_specs=[
            spec(rows // G, 0), spec(rows // G, 0),
            pl.BlockSpec((2, blocks, width), lambda i: (0, 0, 0)), spec(2 * HALO + 2 * G, 0),
        ],
        out_shape=[
            jax.ShapeDtypeStruct((rows // G, width), jnp.bfloat16),
            jax.ShapeDtypeStruct((rows // G, width), jnp.bfloat16),
            jax.ShapeDtypeStruct((2, blocks, width), jnp.bfloat16),
            jax.ShapeDtypeStruct((2 * HALO + 2 * G, width), jnp.bfloat16),
        ],
        compiler_params=params(60),
        cost_estimate=cost(0),
        name="pool",
    )(*[key] * blocks, *[value] * blocks)


def near_kernel(
    info_ref, q_ref, k_ref, v_ref, k1_ref, v1_ref, pk_ref, pv_ref, pk1_ref, pv1_ref, *refs
):
    out_ref, lse_ref, pack_ref, kx, vx, k1x, v1x, bias_ref = refs[-8:]
    rows, width = q_ref.shape
    heads = width // HD
    ones = jnp.ones((SPAN, HD), jnp.bfloat16)
    pad = jnp.zeros((SPAN - NEAR - 2 * G, HD), jnp.bfloat16)
    lane = lax.broadcasted_iota(jnp.int32, (TILE, HD), 1)
    step = pl.program_id(0)
    for ext, prev, now in ((kx, pk_ref, k_ref), (vx, pv_ref, v_ref), (k1x, pk1_ref, k1_ref), (v1x, pv1_ref, v1_ref)):
        before, count = prev.shape[0], now.shape[0]

        @pl.when(step == 0)
        def _():
            ext[:before, :] = prev[...]

        @pl.when(step > 0)
        def _():
            ext[:before, :] = ext[count : count + before, :]

        ext[before : before + count, :] = now[...]
    block = info_ref[0] + step
    row_cell = lax.broadcasted_iota(jnp.int32, (TILE, SPAN), 0) // G
    row = lax.broadcasted_iota(jnp.int32, (TILE, SPAN), 0)
    at_lane = lax.broadcasted_iota(jnp.int32, (TILE, SPAN), 1)
    for t in range(rows // TILE):
        window = jnp.zeros((TILE, SPAN), jnp.int32)
        for c in range(TILE // G):
            here = info_ref[2 + block * (rows // G) + t * (TILE // G) + c]
            window = jnp.where(row_cell == c, here, window)
        start = info_ref[1] + block * rows + t * TILE
        near_ok = (
            (at_lane >= HALO - start) & (at_lane - HALO <= row)
            & (at_lane // G >= row_cell + WMAX - window)
        )
        mid = at_lane - NEAR - G
        mid_ok = (mid >= -((start // (G * G)) * G)) & (
            mid <= t * (TILE // G) + row_cell - window - 1
        )
        lanes = jnp.where(
            at_lane < NEAR,
            near_ok.astype(jnp.int32),
            jnp.where(at_lane < NEAR + 2 * G, mid_ok.astype(jnp.int32), 0),
        )
        bias_ref[t * TILE : (t + 1) * TILE, :] = jnp.where(lanes == 1, 0.0, -jnp.inf)
    for p in range(heads // CHUNK):
        pack_ref[p] = q_ref[:, p * CHUNK * HD : (p + 1) * CHUNK * HD]
    lses = {}

    def where(job):
        t, h = job
        return slice(t * TILE, (t + 1) * TILE), slice(h * HD, (h + 1) * HD)

    def rows_of(src, src1, job):
        t, _ = job
        _, cols = where(job)
        return jnp.concatenate([src[t * TILE : t * TILE + NEAR, cols], src1[:, cols], pad], axis=0)

    def score(job, _):
        at, cols = where(job)
        return lax.dot_general(
            q_ref[at, cols], rows_of(kx, k1x, job), (((1,), (1,)), ((), ())),
            preferred_element_type=jnp.float32,
        )

    def weigh(job, s):
        at, _ = where(job)
        s = s * SCALE + bias_ref[at, :]
        top = jnp.max(s, axis=1, keepdims=True)
        return top, jnp.exp2(s - top).astype(jnp.bfloat16)

    def finish(job, kept):
        at, _ = where(job)
        t, h = job
        top, w = kept
        values = jnp.concatenate([rows_of(vx, v1x, job), ones], axis=1)
        both = jnp.dot(w, values, preferred_element_type=jnp.float32)
        total = both[:, HD:]
        part = h % CHUNK
        out_ref[h // CHUNK, at, part * HD : (part + 1) * HD] = (both[:, :HD] / total).astype(
            jnp.bfloat16
        )
        lse = top + jnp.log2(total)
        lses[t] = jnp.where(lane == h, lse, lses[t]) if h else lse
        if h == heads - 1:
            lse_ref[at, :] = lses[t]

    staged([(t, h) for t in range(rows // TILE) for h in range(heads)], [score, weigh, finish])


def near(query, key, value, key1, value1, prev, info, first, blocks, before):
    rows, width = query.shape
    block = G * G
    pairs = width // HD // CHUNK
    spec = lambda n: pl.BlockSpec((n, width), lambda i, s: (s[0] + i, 0))
    args = [query, key, value, key1, value1] + [p for p, _, _ in prev]
    specs = [spec(block), spec(block), spec(block), spec(G), spec(G)]
    specs += [pl.BlockSpec((n, width), lambda i, s, at=at: (at, 0)) for _, n, at in prev]
    shapes = [
        jax.ShapeDtypeStruct((pairs, rows, CHUNK * HD), jnp.bfloat16),
        jax.ShapeDtypeStruct((rows, HD), jnp.float32),
        jax.ShapeDtypeStruct((pairs, rows, CHUNK * HD), jnp.bfloat16),
    ]
    aliases = {}
    if before is not None:
        aliases = {len(args) + 1 + i: i for i in range(3)}
        args += list(before)
        specs += [pl.BlockSpec(memory_space=pl.ANY)] * 3
    packed = pl.BlockSpec((pairs, block, CHUNK * HD), lambda i, s: (0, s[0] + i, 0))
    return pl.pallas_call(
        near_kernel,
        grid_spec=pltpu.PrefetchScalarGridSpec(
            num_scalar_prefetch=1,
            grid=(blocks,),
            in_specs=specs,
            out_specs=[packed, pl.BlockSpec((block, HD), lambda i, s: (s[0] + i, 0)), packed],
            scratch_shapes=[
                pltpu.VMEM((HALO + block, width), jnp.bfloat16),
                pltpu.VMEM((HALO + block, width), jnp.bfloat16),
                pltpu.VMEM((2 * G, width), jnp.bfloat16),
                pltpu.VMEM((2 * G, width), jnp.bfloat16),
                pltpu.VMEM((block, SPAN), jnp.float32),
            ],
        ),
        out_shape=shapes,
        input_output_aliases=aliases,
        compiler_params=params(60),
        cost_estimate=cost(0),
        name="near",
    )(jnp.concatenate([jnp.full((1,), first, jnp.int32), info]), *args)


def far_kernel(pair, lim_ref, q_ref, n_ref, lse_ref, k2_ref, v2_ref, cell_ref, *out_refs):
    rows = q_ref.shape[1]
    heads = CHUNK * len(out_refs)
    ones = jnp.ones((k2_ref.shape[1], HD), jnp.bfloat16)
    cell = cell_ref[...]
    limit = lim_ref[0] + pl.program_id(0) * (rows // (G * G))

    def where(job):
        t, h = job
        part = h % CHUNK * HD
        return h // CHUNK, slice(t * TILE, (t + 1) * TILE), slice(part, part + HD), slice(h * HD, (h + 1) * HD)

    def score(job, _):
        p, at, cols, keys = where(job)
        return lax.dot_general(
            q_ref[p, at, cols], k2_ref[0, :, keys], (((1,), (1,)), ((), ())),
            preferred_element_type=jnp.float32,
        )

    def weigh(job, s):
        t, h = job
        _, at, _, _ = where(job)
        last = limit + t * TILE // (G * G)
        s = s * SCALE + jnp.where(cell <= last, 0.0, -jnp.inf)
        lse = lse_ref[at, pair * CHUNK + h : pair * CHUNK + h + 1]
        top = jnp.maximum(jnp.max(s, axis=1, keepdims=True), lse)
        return jnp.exp2(lse - top), jnp.exp2(s - top).astype(jnp.bfloat16)

    def finish(job, kept):
        p, at, cols, keys = where(job)
        part, w = kept
        values = jnp.concatenate([v2_ref[0, :, keys], ones], axis=1)
        both = jnp.dot(w, values, preferred_element_type=jnp.float32)
        summed = both[:, :HD] + n_ref[p, at, cols].astype(jnp.float32) * part
        done = (summed / (both[:, HD:] + part)).astype(jnp.bfloat16)
        out_refs[p][at, cols] = done

    staged([(t, h) for h in range(heads) for t in range(rows // TILE)], [score, weigh, finish])


def far(lim, query, partial, lse, kv2, col, cell, pair, count=1):
    rows, cells = query.shape[1], kv2.shape[1]
    width = CHUNK * HD
    tile = 512
    args = [lim, query, partial, lse, kv2, kv2, cell]
    return pl.pallas_call(
        functools.partial(far_kernel, pair),
        grid_spec=pltpu.PrefetchScalarGridSpec(
            num_scalar_prefetch=1,
            grid=(rows // tile,),
            in_specs=[
                pl.BlockSpec((count, tile, width), lambda i, s: (pair // count, i, 0)),
                pl.BlockSpec((count, tile, width), lambda i, s: (pair // count, i, 0)),
                pl.BlockSpec((tile, HD), lambda i, s: (i, 0)),
                pl.BlockSpec((1, cells, count * width), lambda i, s: (0, 0, col)),
                pl.BlockSpec((1, cells, count * width), lambda i, s: (1, 0, col)),
                pl.BlockSpec((1, cells), lambda i, s: (0, 0)),
            ],
            out_specs=[pl.BlockSpec((tile, width), lambda i, s: (i, 0))] * count,
        ),
        out_shape=[jax.ShapeDtypeStruct((rows, width), jnp.bfloat16)] * count,
        compiler_params=params(60),
        cost_estimate=cost(0),
        name="far",
    )(*args)


def project_kernel(n, has_acc, place_ref, *refs):
    held = [ref[...] for ref in refs[:n]]
    weights = jnp.concatenate([r[...] for r in refs[n : 2 * n]], axis=0)
    total = jnp.dot(jnp.concatenate(held, axis=1), weights, preferred_element_type=jnp.float32)
    if has_acc:
        total = total + refs[2 * n][...]
    refs[-1][...] = total.astype(refs[-1].dtype)


def project(pieces, places, weight, acc, dtype):
    n = len(pieces)
    rows, width = pieces[0].shape
    cols = weight.shape[1]
    tile = 256
    out_spec = pl.BlockSpec((tile, cols), lambda i, s: (i, 0))
    specs = [pl.BlockSpec((tile, width), lambda i, s: (i, 0)) for _ in pieces]
    specs += [pl.BlockSpec((width, cols), lambda i, s, j=j: (s[j], 0)) for j in range(n)]
    args = list(pieces) + [weight] * n
    if acc is not None:
        specs.append(out_spec)
        args.append(acc)
    return pl.pallas_call(
        functools.partial(project_kernel, n, acc is not None),
        grid_spec=pltpu.PrefetchScalarGridSpec(
            num_scalar_prefetch=1,
            grid=(rows // tile,),
            in_specs=specs,
            out_specs=out_spec,
        ),
        out_shape=jax.ShapeDtypeStruct((rows, cols), dtype),
        compiler_params=params(60),
        cost_estimate=cost(0),
        name="project",
    )(jnp.stack(places).astype(jnp.int32), *args)


def local(query, key, value, windows, out_weight):
    rows, width = query.shape
    heads = width // HD
    ny, nz = lax.axis_size("y"), lax.axis_size("z")
    iy, ix, iz = (lax.axis_index(a) for a in CTX)
    ctx = lax.axis_index(CTX)
    coarse = rows // (G * G)

    key1, value1, mine, edge = pool(key, value)

    block = G * G
    upper = rows // block // 2
    ahead = [
        (key, HALO, upper * block // HALO - 1), (value, HALO, upper * block // HALO - 1),
        (key1, G, upper - 1), (value1, G, upper - 1),
    ]
    info = jnp.concatenate([(ctx * rows).reshape(1).astype(jnp.int32), windows])

    other = lax.ppermute(mine, "xh", [(0, 1), (1, 0)])
    part = near(query, key, value, key1, value1, ahead, info, upper, rows // block - upper, None)
    mine, part = lax.optimization_barrier((mine, part))
    x = jnp.concatenate([mine, other], axis=1)[:, None]
    halo = lax.ppermute(edge, CTX, [(i, i + 1) for i in range(lax.axis_size(CTX) - 1)])
    x, halo = lax.optimization_barrier((x, halo))
    a, b = shift(x, "z", 3), shift(x, "z", -3)
    behind = [(halo, HALO, 0), (halo, HALO, 1), (halo, G, 2 * HALO // G), (halo, G, 2 * HALO // G + 1)]
    part = near(query, key, value, key1, value1, behind, info, 0, upper, part)
    x, part = lax.optimization_barrier((x, part))
    x = jnp.concatenate([x, a, b], axis=1)
    c, d = shift(x, "z", 1), shift(x[:, :2], "z", -1)
    x = jnp.concatenate([x, c, d], axis=1)
    zs = (iz + jnp.array([0, -3, 3, -1, -4, 2, 1, -2], jnp.int32)) % nz
    ys = (iy + jnp.array([0, -1, 1, -2], jnp.int32)) % ny
    xs = jnp.stack([ix, 1 - ix])
    cell = (
        ((ys[:, None, None] * 2 + xs[None, None, :]) * nz + zs[None, :, None])[..., None] * coarse
        + jnp.arange(coarse, dtype=jnp.int32)
    ).reshape(1, -1)

    def over_y(part):
        parts = [part] + [shift(part, "y", s) for s in (1, -1, 2)]
        return jnp.concatenate(parts, axis=1).reshape(2, -1, part.shape[-1])

    lim = (ctx * coarse - 2).reshape(1).astype(jnp.int32)
    xl, core = lax.axis_index("xl"), lax.axis_index("core")
    swap = [(0, 1), (1, 0)]
    pairs = heads // CHUNK
    soon = 2
    step = soon * CHUNK * HD
    kv_first = over_y(x[..., :step])
    kv_first, x = lax.optimization_barrier((kv_first, x[..., step:]))
    kv_rest = over_y(x)

    here, there = xl * 2, (1 - xl) * 2
    last = pairs - 1
    own, across, beside, diagonal = [], [], [], []

    def place(kind, i):
        base = here if kind < 2 else there
        return (base + (core if kind % 2 == 0 else 1 - core)) * pairs + i

    def add(which, acc, dtype=jnp.float32):
        sets = (own, beside, across, diagonal)
        pieces, places = [], []
        for kind, i in which:
            pieces.append(sets[kind][i])
            places.append(place(kind, i))
        return project(pieces, places, out_weight, acc, dtype)

    hop = lambda axis, xs: [lax.ppermute(o, axis, swap) for o in xs]

    def attend(n, kv2, col, count=1):
        own.extend(far(lim, part[2], part[0], part[1], kv2, col, cell, n, count))
        across.extend(hop("xl", own[n:]))

    attend(0, kv_first, 0)
    kv_first, own[0] = lax.optimization_barrier((kv_first, own[0]))
    attend(1, kv_first, 1)
    kv_rest, *both = lax.optimization_barrier((kv_rest, *own, across[0]))
    beside += hop("core", both[:2])
    diagonal += hop("core", both[2:])
    attend(2, kv_rest, 0, 2)
    own[2], own[3], across[1] = lax.optimization_barrier((own[2], own[3], across[1]))
    diagonal += hop("core", across[1:2])
    beside += hop("core", own[2:])
    acc = add([(0, 0), (0, 1), (1, 0), (1, 1), (2, 0), (3, 0)], None)
    across[2], acc = lax.optimization_barrier((across[2], acc))
    diagonal += hop("core", across[2:3])
    acc = add([(2, 1), (3, 1), (0, 2), (1, 2), (0, 3), (1, 3), (2, 2)], acc)
    across[3], acc = lax.optimization_barrier((across[3], acc))
    diagonal += hop("core", across[3:])
    return add([(3, 2), (2, 3), (3, 3)], acc, jnp.bfloat16)


def solution(mesh):
    split = Mesh(mesh.devices.reshape(4, 2, 8, 2, 2), CTX + ("xl", "core"))
    rows, cols = CTX, ("xl", "core")
    in_specs = (P(rows, cols), P(rows, cols), P(rows, cols), P(rows), P(None, cols))
    return jax.shard_map(
        local, mesh=split, in_specs=in_specs, out_specs=P(rows, cols), check_vma=False
    )
```

```python
import functools

import jax
import jax.numpy as jnp
from jax import lax
from jax.experimental import pallas as pl
from jax.experimental.pallas import tpu as pltpu
from jax.sharding import Mesh
from jax.sharding import PartitionSpec as P

HD = 128
G = 16
WMAX = 4
HALO = WMAX * G
LOG2E = 1.4426950408889634
SCALE = HD ** (-0.5) * LOG2E
CTX = ("y", "xh", "z")
TILE = 128
NEAR = TILE + HALO
SPAN = 256
CHUNK = 2
MIB = 1024 * 1024
DEPTH = 3


def params(mib):
    return pltpu.CompilerParams(vmem_limit_bytes=mib * MIB)


def cost(micros):
    return pl.CostEstimate(flops=micros * 10**9, bytes_accessed=1000, transcendentals=0)


def shift(x, axis, by):
    n = lax.axis_size(axis)
    return lax.ppermute(x, axis, [(i, (i + by) % n) for i in range(n)])


def staged(jobs, stages):
    kept = {}
    for i in range(len(jobs) + DEPTH * (len(stages) - 1)):
        for n, stage in enumerate(stages):
            j = i - n * DEPTH
            if 0 <= j < len(jobs):
                kept[j] = stage(jobs[j], kept.get(j))


def pool_kernel(*refs):
    k1_ref, v1_ref, far_ref, edge_ref = refs[-4:]
    blocks = (len(refs) - 4) // 2
    rows, width = refs[0].shape
    r = lax.broadcasted_iota(jnp.int32, (rows // G, rows), 0)
    t = lax.broadcasted_iota(jnp.int32, (rows // G, rows), 1)
    pick = jnp.where(t // G == r, 1.0, 0.0).astype(jnp.bfloat16)
    for slot, one in ((0, k1_ref), (1, v1_ref)):
        wholes = []
        for b in range(blocks):
            src = refs[slot * blocks + b]
            sums = jnp.dot(pick, src[...], preferred_element_type=jnp.float32)
            one[b * G : (b + 1) * G, :] = (sums * (1.0 / G)).astype(jnp.bfloat16)
            wholes.append(jnp.sum(sums, axis=0, keepdims=True) * (1.0 / (G * G)))
        far_ref[slot] = jnp.concatenate(wholes, axis=0).astype(jnp.bfloat16)
        edge_ref[slot * HALO : (slot + 1) * HALO, :] = src[rows - HALO :, :]
        edge_ref[2 * HALO + slot * G : 2 * HALO + (slot + 1) * G, :] = one[blocks * G - G :, :]


def pool(key, value):
    rows, width = key.shape
    block = G * G
    blocks = rows // block
    spec = lambda n, b: pl.BlockSpec((n, width), lambda i: (b, 0))
    return pl.pallas_call(
        pool_kernel,
        grid=(1,),
        in_specs=[spec(block, b) for b in range(blocks)] * 2,
        out_specs=[
            spec(rows // G, 0), spec(rows // G, 0),
            pl.BlockSpec((2, blocks, width), lambda i: (0, 0, 0)), spec(2 * HALO + 2 * G, 0),
        ],
        out_shape=[
            jax.ShapeDtypeStruct((rows // G, width), jnp.bfloat16),
            jax.ShapeDtypeStruct((rows // G, width), jnp.bfloat16),
            jax.ShapeDtypeStruct((2, blocks, width), jnp.bfloat16),
            jax.ShapeDtypeStruct((2 * HALO + 2 * G, width), jnp.bfloat16),
        ],
        compiler_params=params(60),
        cost_estimate=cost(0),
        name="pool",
    )(*[key] * blocks, *[value] * blocks)


def near_kernel(
    info_ref, q_ref, k_ref, v_ref, k1_ref, v1_ref, pk_ref, pv_ref, pk1_ref, pv1_ref, *refs
):
    out_ref, lse_ref, pack_ref, kx, vx, k1x, v1x, bias_ref = refs[-8:]
    rows, width = q_ref.shape
    heads = width // HD
    ones = jnp.ones((SPAN, HD), jnp.bfloat16)
    pad = jnp.zeros((SPAN - NEAR - 2 * G, HD), jnp.bfloat16)
    lane = lax.broadcasted_iota(jnp.int32, (TILE, HD), 1)
    step = pl.program_id(0)
    for ext, prev, now in ((kx, pk_ref, k_ref), (vx, pv_ref, v_ref), (k1x, pk1_ref, k1_ref), (v1x, pv1_ref, v1_ref)):
        before, count = prev.shape[0], now.shape[0]

        @pl.when(step == 0)
        def _():
            ext[:before, :] = prev[...]

        @pl.when(step > 0)
        def _():
            ext[:before, :] = ext[count : count + before, :]

        ext[before : before + count, :] = now[...]
    block = info_ref[0] + step
    row_cell = lax.broadcasted_iota(jnp.int32, (TILE, SPAN), 0) // G
    row = lax.broadcasted_iota(jnp.int32, (TILE, SPAN), 0)
    at_lane = lax.broadcasted_iota(jnp.int32, (TILE, SPAN), 1)
    for t in range(rows // TILE):
        window = jnp.zeros((TILE, SPAN), jnp.int32)
        for c in range(TILE // G):
            here = info_ref[2 + block * (rows // G) + t * (TILE // G) + c]
            window = jnp.where(row_cell == c, here, window)
        start = info_ref[1] + block * rows + t * TILE
        near_ok = (
            (at_lane >= HALO - start) & (at_lane - HALO <= row)
            & (at_lane // G >= row_cell + WMAX - window)
        )
        mid = at_lane - NEAR - G
        mid_ok = (mid >= -((start // (G * G)) * G)) & (
            mid <= t * (TILE // G) + row_cell - window - 1
        )
        lanes = jnp.where(
            at_lane < NEAR,
            near_ok.astype(jnp.int32),
            jnp.where(at_lane < NEAR + 2 * G, mid_ok.astype(jnp.int32), 0),
        )
        bias_ref[t * TILE : (t + 1) * TILE, :] = jnp.where(lanes == 1, 0.0, -jnp.inf)
    for p in range(heads // CHUNK):
        pack_ref[p] = q_ref[:, p * CHUNK * HD : (p + 1) * CHUNK * HD]
    lses = {}

    def where(job):
        t, h = job
        return slice(t * TILE, (t + 1) * TILE), slice(h * HD, (h + 1) * HD)

    def rows_of(src, src1, job):
        t, _ = job
        _, cols = where(job)
        return jnp.concatenate([src[t * TILE : t * TILE + NEAR, cols], src1[:, cols], pad], axis=0)

    def score(job, _):
        at, cols = where(job)
        return lax.dot_general(
            q_ref[at, cols], rows_of(kx, k1x, job), (((1,), (1,)), ((), ())),
            preferred_element_type=jnp.float32,
        )

    def weigh(job, s):
        at, _ = where(job)
        s = s * SCALE + bias_ref[at, :]
        top = jnp.max(s, axis=1, keepdims=True)
        return top, jnp.exp2(s - top).astype(jnp.bfloat16)

    def finish(job, kept):
        at, _ = where(job)
        t, h = job
        top, w = kept
        values = jnp.concatenate([rows_of(vx, v1x, job), ones], axis=1)
        both = jnp.dot(w, values, preferred_element_type=jnp.float32)
        total = both[:, HD:]
        part = h % CHUNK
        out_ref[h // CHUNK, at, part * HD : (part + 1) * HD] = (both[:, :HD] / total).astype(
            jnp.bfloat16
        )
        lse = top + jnp.log2(total)
        lses[t] = jnp.where(lane == h, lse, lses[t]) if h else lse
        if h == heads - 1:
            lse_ref[at, :] = lses[t]

    staged([(t, h) for t in range(rows // TILE) for h in range(heads)], [score, weigh, finish])


def near(query, key, value, key1, value1, prev, info, first, blocks, before):
    rows, width = query.shape
    block = G * G
    pairs = width // HD // CHUNK
    spec = lambda n: pl.BlockSpec((n, width), lambda i, s: (s[0] + i, 0))
    args = [query, key, value, key1, value1] + [p for p, _, _ in prev]
    specs = [spec(block), spec(block), spec(block), spec(G), spec(G)]
    specs += [pl.BlockSpec((n, width), lambda i, s, at=at: (at, 0)) for _, n, at in prev]
    shapes = [
        jax.ShapeDtypeStruct((pairs, rows, CHUNK * HD), jnp.bfloat16),
        jax.ShapeDtypeStruct((rows, HD), jnp.float32),
        jax.ShapeDtypeStruct((pairs, rows, CHUNK * HD), jnp.bfloat16),
    ]
    aliases = {}
    if before is not None:
        aliases = {len(args) + 1 + i: i for i in range(3)}
        args += list(before)
        specs += [pl.BlockSpec(memory_space=pl.ANY)] * 3
    packed = pl.BlockSpec((pairs, block, CHUNK * HD), lambda i, s: (0, s[0] + i, 0))
    return pl.pallas_call(
        near_kernel,
        grid_spec=pltpu.PrefetchScalarGridSpec(
            num_scalar_prefetch=1,
            grid=(blocks,),
            in_specs=specs,
            out_specs=[packed, pl.BlockSpec((block, HD), lambda i, s: (s[0] + i, 0)), packed],
            scratch_shapes=[
                pltpu.VMEM((HALO + block, width), jnp.bfloat16),
                pltpu.VMEM((HALO + block, width), jnp.bfloat16),
                pltpu.VMEM((2 * G, width), jnp.bfloat16),
                pltpu.VMEM((2 * G, width), jnp.bfloat16),
                pltpu.VMEM((block, SPAN), jnp.float32),
            ],
        ),
        out_shape=shapes,
        input_output_aliases=aliases,
        compiler_params=params(60),
        cost_estimate=cost(0),
        name="near",
    )(jnp.concatenate([jnp.full((1,), first, jnp.int32), info]), *args)


def far_kernel(pair, lim_ref, q_ref, n_ref, lse_ref, k2_ref, v2_ref, cell_ref, *out_refs):
    rows = q_ref.shape[1]
    heads = CHUNK * len(out_refs)
    ones = jnp.ones((k2_ref.shape[1], HD), jnp.bfloat16)
    cell = cell_ref[...]
    limit = lim_ref[0] + pl.program_id(0) * (rows // (G * G))

    def where(job):
        t, h = job
        part = h % CHUNK * HD
        return h // CHUNK, slice(t * TILE, (t + 1) * TILE), slice(part, part + HD), slice(h * HD, (h + 1) * HD)

    def score(job, _):
        p, at, cols, keys = where(job)
        return lax.dot_general(
            q_ref[p, at, cols], k2_ref[0, :, keys], (((1,), (1,)), ((), ())),
            preferred_element_type=jnp.float32,
        )

    def weigh(job, s):
        t, h = job
        _, at, _, _ = where(job)
        last = limit + t * TILE // (G * G)
        s = s * SCALE + jnp.where(cell <= last, 0.0, -jnp.inf)
        lse = lse_ref[at, pair * CHUNK + h : pair * CHUNK + h + 1]
        top = jnp.maximum(jnp.max(s, axis=1, keepdims=True), lse)
        return jnp.exp2(lse - top), jnp.exp2(s - top).astype(jnp.bfloat16)

    def finish(job, kept):
        p, at, cols, keys = where(job)
        part, w = kept
        values = jnp.concatenate([v2_ref[0, :, keys], ones], axis=1)
        both = jnp.dot(w, values, preferred_element_type=jnp.float32)
        summed = both[:, :HD] + n_ref[p, at, cols].astype(jnp.float32) * part
        done = (summed / (both[:, HD:] + part)).astype(jnp.bfloat16)
        out_refs[p][at, cols] = done

    staged([(t, h) for h in range(heads) for t in range(rows // TILE)], [score, weigh, finish])


def far(lim, query, partial, lse, kv2, col, cell, pair, count=1):
    rows, cells = query.shape[1], kv2.shape[1]
    width = CHUNK * HD
    tile = 512
    args = [lim, query, partial, lse, kv2, kv2, cell]
    return pl.pallas_call(
        functools.partial(far_kernel, pair),
        grid_spec=pltpu.PrefetchScalarGridSpec(
            num_scalar_prefetch=1,
            grid=(rows // tile,),
            in_specs=[
                pl.BlockSpec((count, tile, width), lambda i, s: (pair // count, i, 0)),
                pl.BlockSpec((count, tile, width), lambda i, s: (pair // count, i, 0)),
                pl.BlockSpec((tile, HD), lambda i, s: (i, 0)),
                pl.BlockSpec((1, cells, count * width), lambda i, s: (0, 0, col)),
                pl.BlockSpec((1, cells, count * width), lambda i, s: (1, 0, col)),
                pl.BlockSpec((1, cells), lambda i, s: (0, 0)),
            ],
            out_specs=[pl.BlockSpec((tile, width), lambda i, s: (i, 0))] * count,
        ),
        out_shape=[jax.ShapeDtypeStruct((rows, width), jnp.bfloat16)] * count,
        compiler_params=params(60),
        cost_estimate=cost(0),
        name="far",
    )(*args)


def project_kernel(n, has_acc, place_ref, *refs):
    held = [ref[...] for ref in refs[:n]]
    weights = jnp.concatenate([r[...] for r in refs[n : 2 * n]], axis=0)
    total = jnp.dot(jnp.concatenate(held, axis=1), weights, preferred_element_type=jnp.float32)
    if has_acc:
        total = total + refs[2 * n][...]
    refs[-1][...] = total.astype(refs[-1].dtype)


def project(pieces, places, holders, pairs, weight, acc, dtype):
    n = len(pieces)
    rows, width = pieces[0].shape
    cols = weight.shape[1]
    tile = 256
    out_spec = pl.BlockSpec((tile, cols), lambda i, s: (i, 0))
    specs = [pl.BlockSpec((tile, width), lambda i, s: (i, 0)) for _ in pieces]
    specs += [pl.BlockSpec((width, cols), lambda i, s, k=k, p=p: (s[k] * pairs + p, 0)) for k, p in places]
    args = list(pieces) + [weight] * n
    if acc is not None:
        specs.append(out_spec)
        args.append(acc)
    return pl.pallas_call(
        functools.partial(project_kernel, n, acc is not None),
        grid_spec=pltpu.PrefetchScalarGridSpec(
            num_scalar_prefetch=1,
            grid=(rows // tile,),
            in_specs=specs,
            out_specs=out_spec,
        ),
        out_shape=jax.ShapeDtypeStruct((rows, cols), dtype),
        compiler_params=params(60),
        cost_estimate=cost(0),
        name="project",
    )(holders, *args)


def local(query, key, value, windows, out_weight):
    rows, width = query.shape
    heads = width // HD
    ny, nz = lax.axis_size("y"), lax.axis_size("z")
    iy, ix, iz = (lax.axis_index(a) for a in CTX)
    ctx = lax.axis_index(CTX)
    coarse = rows // (G * G)

    key1, value1, mine, edge = pool(key, value)

    block = G * G
    upper = rows // block // 2
    ahead = [
        (key, HALO, upper * block // HALO - 1), (value, HALO, upper * block // HALO - 1),
        (key1, G, upper - 1), (value1, G, upper - 1),
    ]
    info = jnp.concatenate([(ctx * rows).reshape(1).astype(jnp.int32), windows])

    other = lax.ppermute(mine, "xh", [(0, 1), (1, 0)])
    part = near(query, key, value, key1, value1, ahead, info, upper, rows // block - upper, None)
    mine, part = lax.optimization_barrier((mine, part))
    x = jnp.concatenate([mine, other], axis=1)[:, None]
    halo = lax.ppermute(edge, CTX, [(i, i + 1) for i in range(lax.axis_size(CTX) - 1)])
    x, halo = lax.optimization_barrier((x, halo))
    a, b = shift(x, "z", 3), shift(x, "z", -3)
    behind = [(halo, HALO, 0), (halo, HALO, 1), (halo, G, 2 * HALO // G), (halo, G, 2 * HALO // G + 1)]
    part = near(query, key, value, key1, value1, behind, info, 0, upper, part)
    x, part = lax.optimization_barrier((x, part))
    x = jnp.concatenate([x, a, b], axis=1)
    c, d = shift(x, "z", 1), shift(x[:, :2], "z", -1)
    x = jnp.concatenate([x, c, d], axis=1)
    zs = (iz + jnp.array([0, -3, 3, -1, -4, 2, 1, -2], jnp.int32)) % nz
    ys = (iy + jnp.array([0, -1, 1, -2], jnp.int32)) % ny
    xs = jnp.stack([ix, 1 - ix])
    cell = (
        ((ys[:, None, None] * 2 + xs[None, None, :]) * nz + zs[None, :, None])[..., None] * coarse
        + jnp.arange(coarse, dtype=jnp.int32)
    ).reshape(1, -1)

    def over_y(part):
        parts = [part] + [shift(part, "y", s) for s in (1, -1, 2)]
        return jnp.concatenate(parts, axis=1).reshape(2, -1, part.shape[-1])

    lim = (ctx * coarse - 2).reshape(1).astype(jnp.int32)
    xl, core = lax.axis_index("xl"), lax.axis_index("core")
    swap = [(0, 1), (1, 0)]
    pairs = heads // CHUNK
    soon = 2
    step = soon * CHUNK * HD
    kv_first = over_y(x[..., :step])
    kv_first, x = lax.optimization_barrier((kv_first, x[..., step:]))
    kv_rest = over_y(x)

    here, there = xl * 2, (1 - xl) * 2
    last = pairs - 1
    own, across, beside, diagonal = [], [], [], []

    holders = jnp.stack([here + core, here + 1 - core, there + core, there + 1 - core]).astype(jnp.int32)

    def add(which, acc, dtype=jnp.float32):
        sets = (own, beside, across, diagonal)
        pieces = [sets[kind][i] for kind, i in which]
        return project(pieces, which, holders, pairs, out_weight, acc, dtype)

    hop = lambda axis, xs: [lax.ppermute(o, axis, swap) for o in xs]

    def attend(n, kv2, col, count=1):
        own.extend(far(lim, part[2], part[0], part[1], kv2, col, cell, n, count))
        across.extend(hop("xl", own[n:]))

    attend(0, kv_first, 0)
    kv_first, own[0] = lax.optimization_barrier((kv_first, own[0]))
    attend(1, kv_first, 1)
    kv_rest, *both = lax.optimization_barrier((kv_rest, *own, across[0]))
    beside += hop("core", both[:2])
    diagonal += hop("core", both[2:])
    attend(2, kv_rest, 0, 2)
    own[2], own[3], across[1] = lax.optimization_barrier((own[2], own[3], across[1]))
    diagonal += hop("core", across[1:2])
    beside += hop("core", own[2:])
    acc = add([(0, 0), (0, 1), (1, 0), (1, 1), (2, 0), (3, 0)], None)
    across[2], acc = lax.optimization_barrier((across[2], acc))
    diagonal += hop("core", across[2:3])
    acc = add([(2, 1), (3, 1), (0, 2), (1, 2), (0, 3), (1, 3), (2, 2)], acc)
    across[3], acc = lax.optimization_barrier((across[3], acc))
    diagonal += hop("core", across[3:])
    return add([(3, 2), (2, 3), (3, 3)], acc, jnp.bfloat16)


def solution(mesh):
    split = Mesh(mesh.devices.reshape(4, 2, 8, 2, 2), CTX + ("xl", "core"))
    rows, cols = CTX, ("xl", "core")
    in_specs = (P(rows, cols), P(rows, cols), P(rows, cols), P(rows), P(None, cols))
    return jax.shard_map(
        local, mesh=split, in_specs=in_specs, out_specs=P(rows, cols), check_vma=False
    )
```
